32 devices in a mesh: row: 8 (over z, x), col: 4 (over y, core).
Axes of the slice: x: 2, y: 2, z: 4, core: 2. Of those that a mesh axis runs over, the one named last changes fastest.
Arguments:
- acts: bfloat16 [512, 5120], P('col', 'row'), may hold values from -60 to 60
- out_grads: bfloat16 [512, 13824], P('row', 'col'), may hold values from -0.1237436867076458 to 0.1237436867076458
- momentum: float32 [5120, 13824], P('row', 'col'), may hold values from -200 to 200
- weight: float32 [5120, 13824], P('row', 'col'), may hold values from -0.078125 to 0.078125
Outputs:
- momentum_new: float32 [5120, 13824], P('row', 'col')
- update: bfloat16 [5120, 13824], P('row', 'col')
- weight_new: float32 [5120, 13824], P('row', 'col')
The draws below stay inside these ranges and needn't reach their ends.
All inputs are finite; a program needn't handle non-finite values.
Results may differ from the reference program's by a relative error of at most 0.014.
Values may be sent and summed in bfloat16 or wider, within the bound.
No kernel may reach another device: no remote copies, remote signals or barrier semaphores. Data moves between devices by JAX's collectives and lax.ppermute only.
A program may use at most 192 MiB of HBM per device.

```python
import math
import jax
import jax.numpy as jnp
from jax import lax

D = 5120
F = 13824
TOKENS = 512
N_COL = 4


def draw_acts(key, part):
    key_values = jax.random.fold_in(key, 11)
    key_jitter = jax.random.fold_in(key, 12)
    values = jnp.clip(jax.random.normal(key_values, (TOKENS, D), jnp.float32), -6.0, 6.0)
    jitter = jax.random.uniform(key_jitter, (D,), jnp.float32)
    position = jnp.arange(D, dtype=jnp.float32) / D
    scales = jnp.power(10.0, 0.5 * position + 0.5 * jitter)
    return (values * scales[None, :]).astype(jnp.bfloat16)


def draw_out_grads(key, part):
    key_values = jax.random.fold_in(key, 21)
    key_jitter = jax.random.fold_in(key, 22)
    values = jnp.clip(jax.random.normal(key_values, (TOKENS, F), jnp.float32), -4.0, 4.0)
    jitter = jax.random.uniform(key_jitter, (F,), jnp.float32)
    position = jnp.arange(F, dtype=jnp.float32) / F
    scales = jnp.power(10.0, 0.5 * position + 0.5 * jitter)
    return (values * scales[None, :] * (0.07 / jnp.sqrt(jnp.float32(TOKENS)))).astype(jnp.bfloat16)


def draw_momentum(key, part):
    key_left = jax.random.fold_in(key, 31)
    key_right = jax.random.fold_in(key, 32)
    key_noise = jax.random.fold_in(key, 33)
    key_rowjit = jax.random.fold_in(key, 34)
    key_coljit = jax.random.fold_in(key, 35)
    row_position = jnp.arange(D, dtype=jnp.float32) / D
    col_position = jnp.arange(F, dtype=jnp.float32) / F
    row_jitter = jax.random.uniform(key_rowjit, (D,), jnp.float32)
    col_jitter = jax.random.uniform(key_coljit, (F,), jnp.float32)
    row_scale = jnp.power(10.0, 0.5 * row_position + 0.5 * row_jitter)
    col_scale = jnp.power(10.0, 0.5 * col_position + 0.5 * col_jitter) / 4.6
    left = jnp.clip(jax.random.normal(key_left, (D,), jnp.float32), -4.0, 4.0)
    right = jnp.clip(jax.random.normal(key_right, (F,), jnp.float32), -4.0, 4.0)
    noise = 2.0 * jnp.clip(jax.random.normal(key_noise, (D, F), jnp.float32), -4.0, 4.0)
    left = left * jnp.power(10.0, jnp.cos(4.0 * jnp.pi * row_position)) / 4.6
    planted = 0.65 * left[:, None] * right[None, :]
    return (planted + noise * row_scale[:, None] * col_scale[None, :]).astype(jnp.float32)


def block_scale(key, extent, shards, smallest, largest):
    gain = 1.0
    for dim, shards_of in shards:
        steps = jax.random.uniform(jax.random.fold_in(jax.random.fold_in(key, 6), dim), (shards_of,), jnp.float32, smallest / len(shards), largest / len(shards))
        gain = gain * jnp.repeat(jnp.exp(steps), extent[dim] // shards_of).reshape((-1,) + (1,) * (len(extent) - 1 - dim))
    return gain


def normal_values(key, shape, deviation, bound, shards=(), held_as=jnp.bfloat16):
    values = jax.random.normal(key, shape, jnp.float32) * deviation
    if len(shards) > 0:
        values = block_scale(key, shape, shards, -0.22, 0.18) * values
    return jnp.clip(values, min=-bound, max=bound).astype(held_as)


def setup_inputs(seed: int = 0) -> dict:
    key_of = jax.random.split(jax.random.key(seed), 5)
    acts = draw_acts(jax.random.fold_in(key_of[4], 71), 0)
    out_grads = draw_out_grads(jax.random.fold_in(key_of[4], 71), 0)
    momentum = draw_momentum(jax.random.fold_in(key_of[4], 71), 0)
    weight = normal_values(key_of[3], (D, F), D ** -0.5, 0.078125, ((0, 8), (1, 4)), jnp.float32)
    return dict(acts=acts, out_grads=out_grads, momentum=momentum, weight=weight)


def reference(acts, out_grads, momentum, weight):
    gradient = jnp.dot(acts.T, out_grads, preferred_element_type=jnp.float32)
    momentum_new = 0.95 * momentum + gradient
    blended = gradient + 0.95 * momentum_new
    rounded = blended.astype(jnp.bfloat16)
    block_width = F // N_COL
    gram_sum = jnp.zeros((D, D), jnp.float32)
    for column_block in range(N_COL):
        pieces = rounded[:, column_block * block_width:(column_block + 1) * block_width]
        partial_value = jnp.dot(pieces, pieces.T, preferred_element_type=jnp.float32).astype(jnp.bfloat16)
        partial_value = lax.optimization_barrier(partial_value)
        gram_sum = gram_sum + partial_value.astype(jnp.float32)
    gram = gram_sum.astype(jnp.bfloat16)
    gram_square = jnp.dot(gram, gram, preferred_element_type=jnp.float32)
    schatten = jnp.sqrt(jnp.sum(gram_square * gram_square) + 1e-06)
    square_root = jnp.sqrt(schatten)
    fourth_root = jnp.sqrt(square_root)
    poly = (-4.775 * gram.astype(jnp.float32) / square_root + 2.0315 * gram_square / schatten).astype(jnp.bfloat16)
    product = jnp.dot(poly, rounded, preferred_element_type=jnp.float32)
    orthogonal = (3.4445 * rounded.astype(jnp.float32) + product) / fourth_root
    factor = math.sqrt(D)
    update = (factor * orthogonal).astype(jnp.bfloat16)
    weight_new = 0.998 * weight - 0.02 * factor * orthogonal
    return (momentum_new, update, weight_new)
```

```python
import functools
import math

import jax
import jax.numpy as jnp
from jax import lax
from jax.experimental import pallas as pl
from jax.experimental.pallas import tpu as pltpu
from jax.sharding import PartitionSpec as P

F32 = jnp.float32
BF16 = jnp.bfloat16


def general_body(acts, out_grads, momentum, weight):
    token_acts = lax.all_gather(acts, "col", axis=0, tiled=True)
    token_grads = lax.all_gather(out_grads, "row", axis=0, tiled=True)
    gradient = lax.dot_general(token_acts, token_grads, (((0,), (0,)), ((), ())), preferred_element_type=F32)
    momentum_new = 0.95 * momentum + gradient
    blended = gradient + 0.95 * momentum_new
    rounded = blended.astype(BF16)
    col_panel = lax.all_gather(rounded, "row", axis=0, tiled=True)
    gram_tile = lax.psum_scatter(
        lax.dot_general(col_panel, rounded, (((1,), (1,)), ((), ())), preferred_element_type=F32).astype(BF16),
        "col",
        scatter_dimension=0,
        tiled=True,
    )
    gram_cols = lax.all_gather(gram_tile, "col", axis=0, tiled=True)
    gram_rows = lax.all_gather(gram_tile, "row", axis=1, tiled=True)
    gram_square = jnp.dot(gram_rows, gram_cols, preferred_element_type=F32)
    total_sum = lax.psum(jnp.sum(gram_square * gram_square), ("row", "col"))
    schatten = jnp.sqrt(total_sum + 1e-06)
    square_root = jnp.sqrt(schatten)
    fourth_root = jnp.sqrt(square_root)
    poly_tile = (-4.775 * gram_tile.astype(F32) / square_root + 2.0315 * gram_square / schatten).astype(BF16)
    poly_cols = lax.all_gather(poly_tile, "col", axis=0, tiled=True)
    product = lax.dot_general(poly_cols, col_panel, (((0,), (0,)), ((), ())), preferred_element_type=F32)
    orthogonal = (3.4445 * rounded.astype(F32) + product) / fourth_root
    factor = math.sqrt(col_panel.shape[0])
    update = (factor * orthogonal).astype(BF16)
    weight_new = 0.998 * weight - 0.02 * factor * orthogonal
    return (momentum_new, update, weight_new)


BLOCKS = 8
TILES = 9
PARTS = 3


def row_shift(value, step):
    return lax.ppermute(value, "row", [(i, (i + step) % BLOCKS) for i in range(BLOCKS)])


def swap(value, axis, bit):
    size = 8 if axis == "row" else 4
    return lax.ppermute(value, axis, [(i, i ^ bit) for i in range(size)])


def take(value, dim, index):
    return lax.dynamic_index_in_dim(value, index, dim, keepdims=False)


def halve(value, dim, mine, axis, bit):
    received = swap(take(value, dim, 1 - mine), axis, bit)
    return (take(value, dim, mine).astype(F32) + received.astype(F32)).astype(BF16)


def tile_blocks(step):
    part = step // 12
    group = (step % 12) // 3
    tile = part * 3 + step % 3
    second = (tile >= 5).astype(jnp.int32)
    row = lax.rem(group + tile - second, 8)
    column = lax.rem(group + 4 * second, 8)
    return row, column


def product_kernel(group_ref, x_ref, t0_ref, t1_ref, t2_ref, y_ref, z_ref, dot_ref, ybf_ref):
    second_pass = pl.program_id(0)
    step = pl.program_id(1)
    row, column = tile_blocks(step)
    group = group_ref[0]
    a = lax.rem(row - group + 8, 8)
    b = lax.rem(column - group + 8, 8)

    @pl.when((second_pass == 0) & (step == 0))
    def _():
        y_ref[...] = jnp.zeros_like(y_ref)
        z_ref[...] = jnp.zeros_like(z_ref)

    def apply(tile_ref, source, target):
        target[b] += jnp.dot(source[a], tile_ref[0], preferred_element_type=F32)

        @pl.when(a != b)
        def _():
            target[a] += lax.dot_general(source[b], tile_ref[0], (((1,), (1,)), ((), ())), preferred_element_type=F32)

    for part, tile_ref in enumerate((t0_ref, t1_ref, t2_ref)):
        @pl.when((step // 12 == part) & (second_pass == 0))
        def _():
            apply(tile_ref, x_ref, y_ref)

        @pl.when((step // 12 == part) & (second_pass == 1))
        def _():
            apply(tile_ref, ybf_ref, z_ref)

    @pl.when((second_pass == 0) & (step == 35))
    def _():
        ybf_ref[...] = y_ref[...].astype(BF16)

    @pl.when((second_pass == 1) & (step == 35))
    def _():
        dot_ref[...] = jnp.sum(y_ref[...] * z_ref[...], axis=0).sum(axis=0, keepdims=True)


def products(group, x, tiles):
    blocks, width, rows = x.shape
    def tile_spec(part):
        return pl.BlockSpec((1, rows, rows), lambda p, i, g: (jnp.clip(i - 12 * part, 0, 11), 0, 0))
    whole = pl.BlockSpec((blocks, width, rows), lambda p, i, g: (0, 0, 0))
    return pl.pallas_call(
        product_kernel,
        out_shape=(
            jax.ShapeDtypeStruct(x.shape, F32),
            jax.ShapeDtypeStruct(x.shape, F32),
            jax.ShapeDtypeStruct((1, rows), F32),
        ),
        grid_spec=pltpu.PrefetchScalarGridSpec(
            num_scalar_prefetch=1,
            grid=(2, 36),
            in_specs=[whole, tile_spec(0), tile_spec(1), tile_spec(2)],
            out_specs=(whole, whole, pl.BlockSpec((1, rows), lambda p, i, g: (0, 0))),
            scratch_shapes=[pltpu.VMEM(x.shape, BF16)],
        ),
        compiler_params=pltpu.CompilerParams(
            dimension_semantics=("arbitrary", "arbitrary"), vmem_limit_bytes=60 * 2**20
        ),
        cost_estimate=pl.CostEstimate(
            flops=2 * 2 * 64 * width * rows * rows, bytes_accessed=2 * 36 * rows * rows * 2, transcendentals=0
        ),
    )(group, x, *tiles)


def gather_part(mine, order, place):
    dims = {"x": 0, "k": 1, "y": 3, "zh": 4, "zl": 5}
    moves = {"x": ("row", 1), "zl": ("row", 2), "zh": ("row", 4), "y": ("col", 2), "k": ("col", 1)}
    count, e, rows = mine.shape
    start = [place["x"], place["k"], 0, place["y"], place["zh"], place["zl"], 0, 0]
    buffer = jnp.zeros((2, 2, count, 2, 2, 2, e, rows), BF16)
    current = mine.reshape(1, 1, count, 1, 1, 1, e, rows)
    buffer = lax.dynamic_update_slice(buffer, current, start)
    for name in order:
        dim = dims[name]
        received = swap(current, *moves[name])
        there = list(start)
        there[dim] = 1 - place[name]
        buffer = lax.dynamic_update_slice(buffer, received, there)
        start[dim] = 0
        sizes = list(current.shape)
        sizes[dim] = 2
        current = lax.dynamic_slice(buffer, start, sizes)
    return current


def fast_body(acts, out_grads, momentum, weight):
    row, col = lax.axis_index("row"), lax.axis_index("col")
    z, x, y, core = row // 2, row % 2, col // 2, col % 2
    place = {"x": x, "k": core, "y": y, "zh": z // 2, "zl": z % 2}
    rows, cols = momentum.shape
    quarter = cols // 4
    half = quarter // 2
    e = rows // 8
    group = 2 * x + core

    token_acts = lax.all_gather(acts, "col", axis=0, tiled=True)
    token_grads = lax.all_gather(out_grads, "row", axis=0, tiled=True)
    gradient = lax.dot_general(token_acts, token_grads, (((0,), (0,)), ((), ())), preferred_element_type=F32)
    momentum_new = 0.95 * momentum + gradient
    rounded = (gradient + 0.95 * momentum_new).astype(BF16)
    pieces = rounded.T.reshape(4, quarter, rows)

    panel = jnp.zeros((BLOCKS, 2, quarter, rows), BF16)
    for step in range(4):
        piece = take(pieces, 0, (z + step) % 4)
        if step:
            piece = row_shift(piece, 2 * step)
        source = 2 * ((z - step + 4) % 4)
        beside = swap(piece, "row", 1)
        for block, value in ((source + x, piece), (source + 1 - x, beside)):
            j = (block - group + 8) % 8
            panel = lax.dynamic_update_slice(panel, value[None, None], (j, 0, 0, 0))
            panel = lax.dynamic_update_slice(panel, swap(value, "col", 1)[None, None], (j, 1, 0, 0))
    deep = panel.reshape(BLOCKS, 2 * quarter, rows)

    def tile(i, j):
        return lax.dot_general(deep[i], deep[j], (((0,), (0,)), ((), ())), preferred_element_type=F32).astype(BF16)

    first = jnp.stack([tile(i, 0) for i in range(5)]).reshape(5, 2, 2, 2, e, rows)
    last = jnp.stack([tile(i, 4) for i in range(4, 8)]).reshape(4, 2, 2, 2, e, rows)
    first = halve(first, 1, y, "col", 2)
    last = halve(last, 3, place["zl"], "row", 2)
    first = halve(first, 2, place["zl"], "row", 2)
    last = halve(last, 2, place["zh"], "row", 4)
    first = halve(first, 1, place["zh"], "row", 4)
    last = halve(last, 1, y, "col", 2)
    mine = jnp.concatenate([first, last])

    orders = (("zh", "zl", "y", "x", "k"), ("y", "x", "zh", "zl", "k"), ("x", "zh", "zl", "y", "k"))
    tiles = [
        gather_part(mine[3 * part : 3 * part + 3], order, place).reshape(12, rows, rows)
        for part, order in enumerate(orders)
    ]

    own = lax.dynamic_slice(panel, (0, 0, x * half, 0), (BLOCKS, 1, half, rows))[:, 0]
    one, three, lanes = products(group.astype(jnp.int32).reshape(1), own, tiles)
    total_sum = lax.psum(jnp.sum(lanes), ("row", "col"))
    schatten = jnp.sqrt(total_sum + 1e-06)
    square_root = jnp.sqrt(schatten)
    fourth_root = jnp.sqrt(square_root)
    factor = math.sqrt(rows * BLOCKS)
    update_t = (
        (3.4445 * own.astype(F32) - (4.775 / square_root) * one + (2.0315 / schatten) * three) * (factor / fourth_root)
    ).astype(BF16)

    home = jnp.zeros((BLOCKS, half, rows), BF16)
    for step in range(BLOCKS):
        value = take(update_t, 0, (row + step - group + 8) % 8)
        if step:
            value = row_shift(value, step)
        home = lax.dynamic_update_slice(home, value[None], ((row - step + 8) % 8, 0, 0))
    update = home.reshape(cols, rows).T
    weight_new = 0.998 * weight - 0.02 * update.astype(F32)
    return (momentum_new, update, weight_new)


def solution(mesh):
    spec = P("row", "col")
    in_specs = (P("col", "row"), spec, spec, spec)
    fast = mesh.shape["row"] == 8 and mesh.shape["col"] == 4
    body = fast_body if fast else general_body
    return jax.shard_map(body, mesh=mesh, in_specs=in_specs, out_specs=(spec, spec, spec), check_vma=False)
```

```python
import functools
import math

import jax
import jax.numpy as jnp
from jax import lax
from jax.experimental import pallas as pl
from jax.experimental.pallas import tpu as pltpu
from jax.sharding import PartitionSpec as P

F32 = jnp.float32
BF16 = jnp.bfloat16


def general_body(acts, out_grads, momentum, weight):
    token_acts = lax.all_gather(acts, "col", axis=0, tiled=True)
    token_grads = lax.all_gather(out_grads, "row", axis=0, tiled=True)
    gradient = lax.dot_general(token_acts, token_grads, (((0,), (0,)), ((), ())), preferred_element_type=F32)
    momentum_new = 0.95 * momentum + gradient
    blended = gradient + 0.95 * momentum_new
    rounded = blended.astype(BF16)
    col_panel = lax.all_gather(rounded, "row", axis=0, tiled=True)
    gram_tile = lax.psum_scatter(
        lax.dot_general(col_panel, rounded, (((1,), (1,)), ((), ())), preferred_element_type=F32).astype(BF16),
        "col",
        scatter_dimension=0,
        tiled=True,
    )
    gram_cols = lax.all_gather(gram_tile, "col", axis=0, tiled=True)
    gram_rows = lax.all_gather(gram_tile, "row", axis=1, tiled=True)
    gram_square = jnp.dot(gram_rows, gram_cols, preferred_element_type=F32)
    total_sum = lax.psum(jnp.sum(gram_square * gram_square), ("row", "col"))
    schatten = jnp.sqrt(total_sum + 1e-06)
    square_root = jnp.sqrt(schatten)
    fourth_root = jnp.sqrt(square_root)
    poly_tile = (-4.775 * gram_tile.astype(F32) / square_root + 2.0315 * gram_square / schatten).astype(BF16)
    poly_cols = lax.all_gather(poly_tile, "col", axis=0, tiled=True)
    product = lax.dot_general(poly_cols, col_panel, (((0,), (0,)), ((), ())), preferred_element_type=F32)
    orthogonal = (3.4445 * rounded.astype(F32) + product) / fourth_root
    factor = math.sqrt(col_panel.shape[0])
    update = (factor * orthogonal).astype(BF16)
    weight_new = 0.998 * weight - 0.02 * factor * orthogonal
    return (momentum_new, update, weight_new)


BLOCKS = 8
PIECES = 5
MOVES = {"x": ("row", 1), "zl": ("row", 2), "zh": ("row", 4), "y": ("col", 2), "k": ("col", 1)}
REDUCE = (("y", "zl"), ("zl", "y"), ("zl", "y"))
GATHER = (("zl", "y", "x"), ("zl", "x", "y"), ("x", "y", "zl"))


def row_shift(value, step):
    return lax.ppermute(value, "row", [(i, (i + step) % BLOCKS) for i in range(BLOCKS)])


def swap(value, name):
    axis, bit = MOVES[name]
    size = 8 if axis == "row" else 4
    return lax.ppermute(value, axis, [(i, i ^ bit) for i in range(size)])


def take(value, dim, index):
    return lax.dynamic_index_in_dim(value, index, dim, keepdims=False)


def reduce_part(tiles, order, place):
    left = ["y", "zl"]
    for name in order:
        dim = 1 + left.index(name)
        left.remove(name)
        received = swap(take(tiles, dim, 1 - place[name]), name)
        tiles = (take(tiles, dim, place[name]).astype(F32) + received.astype(F32)).astype(BF16)
    return (tiles.astype(F32) + swap(tiles, "zh").astype(F32)).astype(BF16)


def gather_part(mine, order):
    mine = jnp.stack([mine, swap(mine, order[0])])
    held = [mine]
    for name in order[1:]:
        held = held + [swap(value, name) for value in held]
    return held + [swap(jnp.stack(held), "k")]


def entry_kernel(acts_ref, momentum_ref, *refs):
    grads_refs, (new_ref, turned_ref) = refs[:-2], refs[-2:]
    grads = jnp.concatenate([ref[...] for ref in grads_refs])
    gradient = jnp.dot(acts_ref[...], grads, preferred_element_type=F32)
    momentum_new = 0.95 * momentum_ref[...] + gradient
    new_ref[...] = momentum_new
    turned_ref[...] = (gradient + 0.95 * momentum_new).T.astype(BF16)


def entry(acts_t, momentum, grads):
    rows, cols = momentum.shape
    tokens = acts_t.shape[1]
    width = cols // 9
    across = pl.BlockSpec((rows, width), lambda i: (0, i))
    return pl.pallas_call(
        entry_kernel,
        out_shape=(jax.ShapeDtypeStruct((rows, cols), F32), jax.ShapeDtypeStruct((cols, rows), BF16)),
        grid=(9,),
        in_specs=[pl.BlockSpec((rows, tokens), lambda i: (0, 0)), across]
        + [pl.BlockSpec((value.shape[0], width), lambda i: (0, i)) for value in grads],
        out_specs=(across, pl.BlockSpec((width, rows), lambda i: (i, 0))),
        compiler_params=pltpu.CompilerParams(vmem_limit_bytes=40 * 2**20),
        cost_estimate=pl.CostEstimate(
            flops=2 * rows * cols * tokens, bytes_accessed=rows * cols * 10 + tokens * cols * 2, transcendentals=0
        ),
    )(acts_t, momentum, *grads)


def finish_kernel(home_ref, weight_ref, update_ref, new_ref):
    update = home_ref[...].astype(F32).T
    update_ref[...] = update.astype(BF16)
    new_ref[...] = 0.998 * weight_ref[...] - 0.02 * update


def finish(home, weight):
    rows, cols = weight.shape
    width = cols // 9
    across = pl.BlockSpec((rows, width), lambda i: (0, i))
    return pl.pallas_call(
        finish_kernel,
        out_shape=(jax.ShapeDtypeStruct((rows, cols), BF16), jax.ShapeDtypeStruct((rows, cols), F32)),
        grid=(9,),
        in_specs=[pl.BlockSpec((width, rows), lambda i: (i, 0)), across],
        out_specs=(across, across),
        compiler_params=pltpu.CompilerParams(vmem_limit_bytes=40 * 2**20),
        cost_estimate=pl.CostEstimate(flops=4 * rows * cols, bytes_accessed=rows * cols * 12, transcendentals=0),
    )(home, weight)


def apply_near(source, tiles, total, blocks, first, last):
    rows = total.shape[2]
    depth = (last - first) * rows

    def near(b, _):
        start = pl.multiple_of((b + first) * rows, 128)
        own = pl.multiple_of(b * rows, 128)
        total[b] += jnp.dot(
            source[:, pl.ds(start, depth)],
            tiles[b, first:last].reshape(depth, rows),
            preferred_element_type=F32,
        )
        for d in range(max(first, 1), last):
            total[lax.rem(b + d, BLOCKS)] += lax.dot_general(
                source[:, pl.ds(own, rows)],
                tiles[b, d].reshape(rows, rows),
                (((1,), (1,)), ((), ())),
                preferred_element_type=F32,
            )
        return 0

    lax.fori_loop(*blocks, near, 0)


def apply_far(source, fours, total):
    rows = total.shape[2]

    def far(b, _):
        start = pl.multiple_of(b * rows, 128)
        other = pl.multiple_of((b + 4) * rows, 128)
        tile = fours[b].reshape(rows, rows)
        total[b] += jnp.dot(source[:, pl.ds(other, rows)], tile, preferred_element_type=F32)
        total[b + 4] += lax.dot_general(
            source[:, pl.ds(start, rows)], tile, (((1,), (1,)), ((), ())), preferred_element_type=F32
        )
        return 0

    lax.fori_loop(0, BLOCKS // 2, far, 0)


def load_tiles(place, part, pieces, tiles, fours, sem):
    for index in range(8):
        for inner in range(2):
            flips = (inner, index & 1, (index >> 1) & 1, index >> 2)
            there = {
                name: 1 - place[name] if flip else place[name] for name, flip in zip(GATHER[part] + ("k",), flips)
            }
            b = 2 * there["x"] + there["k"]
            e = 2 * there["y"] + there["zl"]
            piece = pieces[index].at[inner] if index < 4 else pieces[4].at[index - 4, inner]
            if part < 2:
                pltpu.make_async_copy(piece, tiles.at[b + 4 * part, pl.ds(0, 3), e], sem.at[part]).start()
            else:
                pltpu.make_async_copy(piece.at[0], tiles.at[b, 3, e], sem.at[2]).start()
                pltpu.make_async_copy(piece.at[1], tiles.at[b + 4, 3, e], sem.at[2]).start()
                pltpu.make_async_copy(piece.at[2], fours.at[b, e], sem.at[3]).start()
    if part < 2:
        block = tiles.at[pl.ds(4 * part, 4), pl.ds(0, 3)]
        return [pltpu.make_async_copy(block, block, sem.at[part])]
    block = tiles.at[:, 3]
    return [pltpu.make_async_copy(block, block, sem.at[2]), pltpu.make_async_copy(fours, fours, sem.at[3])]


def load_columns(place, panel_ref, source, sem):
    width = source.shape[0]
    rows = panel_ref.shape[3]
    group = 2 * place["x"] + place["k"]
    copies = []
    for b in range(BLOCKS + 3):
        j = lax.rem(b - group + 2 * BLOCKS, BLOCKS)
        block = panel_ref.at[j, 0, pl.ds(pl.multiple_of(place["x"] * width, 16), width)]
        copies.append(pltpu.make_async_copy(block, source.at[:, pl.ds(b * rows, rows)], sem.at[b]))
        copies[-1].start()
    return copies


def places_of(place_ref):
    return {name: place_ref[i] for i, name in enumerate(("x", "k", "y", "zh", "zl"))}


def product_kernel(place_ref, panel_ref, *refs):
    parts, (y_ref, z_ref, dot_ref), scratch = refs[: 3 * PIECES], refs[3 * PIECES : 3 * PIECES + 3], refs[3 * PIECES + 3 :]
    source, tiles, fours, total, tile_sem, x_sem, out_sem = scratch
    rows = total.shape[2]
    place = places_of(place_ref)
    columns = load_columns(place, panel_ref, source, x_sem)
    arrivals = [
        load_tiles(place, part, parts[PIECES * part : PIECES * part + PIECES], tiles, fours, tile_sem)
        for part in range(3)
    ]
    total[...] = jnp.zeros_like(total)
    for wait in columns + arrivals[0]:
        wait.wait()
    apply_near(source, tiles, total, (0, 4), 0, 3)
    for wait in arrivals[1]:
        wait.wait()
    apply_near(source, tiles, total, (4, 8), 0, 3)
    for wait in arrivals[2]:
        wait.wait()
    apply_near(source, tiles, total, (0, BLOCKS), 3, 4)
    apply_far(source, fours, total)
    out = pltpu.make_async_copy(total, y_ref, out_sem)
    out.start()
    for b in range(BLOCKS + 3):
        source[:, b * rows : (b + 1) * rows] = total[b % BLOCKS].astype(BF16)
    out.wait()
    total[...] = jnp.zeros_like(total)
    apply_near(source, tiles, total, (0, BLOCKS), 0, 4)
    apply_far(source, fours, total)
    out = pltpu.make_async_copy(total, z_ref, out_sem)
    out.start()
    lanes = jnp.zeros((1, rows), F32)
    for b in range(BLOCKS):
        lanes += jnp.sum(source[:, b * rows : (b + 1) * rows].astype(F32) * total[b], axis=0, keepdims=True)
    dot_ref[...] = jnp.broadcast_to(lanes, dot_ref.shape)
    out.wait()


def products(place, panel, parts):
    blocks, _, quarter, rows = panel.shape
    width = quarter // 2
    e = rows // 4
    anywhere = pl.BlockSpec(memory_space=pl.ANY)
    whole = jax.ShapeDtypeStruct((blocks, width, rows), F32)
    return pl.pallas_call(
        product_kernel,
        out_shape=(whole, whole, jax.ShapeDtypeStruct((8, rows), F32)),
        in_specs=[pl.BlockSpec(memory_space=pltpu.SMEM)] + [anywhere] * (1 + len(parts)),
        out_specs=(anywhere, anywhere, pl.BlockSpec(memory_space=pltpu.VMEM)),
        scratch_shapes=[
            pltpu.VMEM((width, (blocks + 3) * rows), BF16),
            pltpu.VMEM((blocks, 4, 4, e, rows), BF16),
            pltpu.VMEM((blocks // 2, 4, e, rows), BF16),
            pltpu.VMEM((blocks, width, rows), F32),
            pltpu.SemaphoreType.DMA((4,)),
            pltpu.SemaphoreType.DMA((blocks + 3,)),
            pltpu.SemaphoreType.DMA,
        ],
        compiler_params=pltpu.CompilerParams(vmem_limit_bytes=60 * 2**20),
        cost_estimate=pl.CostEstimate(
            flops=2 * 2 * 64 * width * rows * rows, bytes_accessed=2 * 36 * rows * rows, transcendentals=0
        ),
    )(place, panel, *parts)


def fast_body(acts, out_grads, momentum, weight):
    row, col = lax.axis_index("row"), lax.axis_index("col")
    z, x, y, core = row // 2, row % 2, col // 2, col % 2
    place = {"x": x, "k": core, "y": y, "zh": z // 2, "zl": z % 2}
    rows, cols = momentum.shape
    quarter = cols // 4
    half = quarter // 2
    e = rows // 4
    group = 2 * x + core

    along = {0: out_grads, 2: swap(out_grads, "zl"), 4: swap(out_grads, "zh")}
    along[6] = swap(along[4], "zl")
    along |= {bits + 1: swap(value, "x") for bits, value in along.items()}
    token_acts = jnp.zeros((4, *acts.shape), BF16)
    for bit in range(4):
        value = lax.ppermute(acts, "col", [(i, i ^ bit) for i in range(4)]) if bit else acts
        token_acts = lax.dynamic_update_slice(token_acts, value[None], (col ^ bit, 0, 0))
    token_acts = token_acts.reshape(BLOCKS, -1, rows)
    acts_t = jnp.concatenate([take(token_acts, 0, row ^ bits) for bits in along]).T
    momentum_new, turned = entry(acts_t, momentum, list(along.values()))
    pieces = turned.reshape(4, quarter, rows)

    panel = jnp.zeros((BLOCKS, 2, quarter, rows), BF16)
    for step in range(4):
        piece = take(pieces, 0, (z + step) % 4)
        if step:
            piece = row_shift(piece, 2 * step)
        source = 2 * ((z - step + 4) % 4)
        beside = swap(piece, "x")
        for block, value in ((source + x, piece), (source + 1 - x, beside)):
            j = (block - group + 8) % 8
            panel = lax.dynamic_update_slice(panel, value[None, None], (j, 0, 0, 0))
            panel = lax.dynamic_update_slice(panel, swap(value, "k")[None, None], (j, 1, 0, 0))
    deep = panel.reshape(BLOCKS, 2 * quarter, rows)

    def tile(deep, i, j):
        return lax.dot_general(deep[i], deep[j], (((0,), (0,)), ((), ())), preferred_element_type=F32).astype(BF16)

    wanted = (((0, 0), (1, 0), (2, 0)), ((4, 4), (5, 4), (6, 4)), ((3, 0), (7, 4), (4, 0)))
    parts = []
    for which in range(3):
        tiles = jnp.stack([tile(deep, i, j) for i, j in wanted[which]]).reshape(3, 2, 2, e, rows)
        deep, tiles = lax.optimization_barrier((deep, tiles))
        parts += gather_part(reduce_part(tiles, REDUCE[which], place), GATHER[which])

    places = jnp.stack([place[name] for name in ("x", "k", "y", "zh", "zl")]).astype(jnp.int32)
    one, two, lanes = products(places, panel, parts)
    total_sum = jnp.broadcast_to(jnp.sum(lanes[0]), (8, 128))
    total_sum = total_sum + sum(row_shift(total_sum, step) for step in range(1, 8))
    total_sum = total_sum + sum(
        lax.ppermute(total_sum, "col", [(i, i ^ bit) for i in range(4)]) for bit in range(1, 4)
    )
    schatten = jnp.sqrt(total_sum[0, 0] + 1e-06)
    square_root = jnp.sqrt(schatten)
    scale = math.sqrt(rows * BLOCKS) / jnp.sqrt(square_root)

    home = jnp.zeros((BLOCKS, half, rows), BF16)
    own = lax.dynamic_slice(panel, (0, 0, x * half, 0), (BLOCKS, 1, half, rows))[:, 0]
    for step in range(BLOCKS):
        there = (row + step) % 8
        value = (
            3.4445 * take(own, 0, (there - group + 8) % 8).astype(F32)
            - (4.775 / square_root) * take(one, 0, there)
            + (2.0315 / schatten) * take(two, 0, there)
        )
        value = (scale * value).astype(BF16)
        if step:
            value = row_shift(value, step)
        home = lax.dynamic_update_slice(home, value[None], ((row - step + 8) % 8, 0, 0))
    update, weight_new = finish(home.reshape(cols, rows), weight)
    return (momentum_new, update, weight_new)


def solution(mesh):
    spec = P("row", "col")
    in_specs = (P("col", "row"), spec, spec, spec)
    fast = mesh.shape["row"] == 8 and mesh.shape["col"] == 4
    body = fast_body if fast else general_body
    return jax.shard_map(body, mesh=mesh, in_specs=in_specs, out_specs=(spec, spec, spec), check_vma=False)
```

```python
import functools
import math

import jax
import jax.numpy as jnp
from jax import lax
from jax.experimental import pallas as pl
from jax.experimental.pallas import tpu as pltpu
from jax.sharding import PartitionSpec as P

F32 = jnp.float32
BF16 = jnp.bfloat16


def general_body(acts, out_grads, momentum, weight):
    token_acts = lax.all_gather(acts, "col", axis=0, tiled=True)
    token_grads = lax.all_gather(out_grads, "row", axis=0, tiled=True)
    gradient = lax.dot_general(token_acts, token_grads, (((0,), (0,)), ((), ())), preferred_element_type=F32)
    momentum_new = 0.95 * momentum + gradient
    blended = gradient + 0.95 * momentum_new
    rounded = blended.astype(BF16)
    col_panel = lax.all_gather(rounded, "row", axis=0, tiled=True)
    gram_tile = lax.psum_scatter(
        lax.dot_general(col_panel, rounded, (((1,), (1,)), ((), ())), preferred_element_type=F32).astype(BF16),
        "col",
        scatter_dimension=0,
        tiled=True,
    )
    gram_cols = lax.all_gather(gram_tile, "col", axis=0, tiled=True)
    gram_rows = lax.all_gather(gram_tile, "row", axis=1, tiled=True)
    gram_square = jnp.dot(gram_rows, gram_cols, preferred_element_type=F32)
    total_sum = lax.psum(jnp.sum(gram_square * gram_square), ("row", "col"))
    schatten = jnp.sqrt(total_sum + 1e-06)
    square_root = jnp.sqrt(schatten)
    fourth_root = jnp.sqrt(square_root)
    poly_tile = (-4.775 * gram_tile.astype(F32) / square_root + 2.0315 * gram_square / schatten).astype(BF16)
    poly_cols = lax.all_gather(poly_tile, "col", axis=0, tiled=True)
    product = lax.dot_general(poly_cols, col_panel, (((0,), (0,)), ((), ())), preferred_element_type=F32)
    orthogonal = (3.4445 * rounded.astype(F32) + product) / fourth_root
    factor = math.sqrt(col_panel.shape[0])
    update = (factor * orthogonal).astype(BF16)
    weight_new = 0.998 * weight - 0.02 * factor * orthogonal
    return (momentum_new, update, weight_new)


BLOCKS = 8
STRIPS = ((0, 4), (4, 9))
PIECES = 5
MOVES = {"x": ("row", 1), "zl": ("row", 2), "zh": ("row", 4), "y": ("col", 2), "k": ("col", 1)}
REDUCE = (("y", "zl"), ("zl", "y"), ("zl", "y"))
GATHER = (("x", "y", "zl"), ("zl", "y", "x"), ("zl", "x", "y"))


def row_shift(value, step):
    return lax.ppermute(value, "row", [(i, (i + step) % BLOCKS) for i in range(BLOCKS)])


def swap(value, name):
    axis, bit = MOVES[name]
    size = 8 if axis == "row" else 4
    return lax.ppermute(value, axis, [(i, i ^ bit) for i in range(size)])


def take(value, dim, index):
    return lax.dynamic_index_in_dim(value, index, dim, keepdims=False)


def halve(tiles, dim, name, place):
    received = swap(take(tiles, dim, 1 - place[name]), name)
    return (take(tiles, dim, place[name]).astype(F32) + received.astype(F32)).astype(BF16)


def after(value, *others):
    return lax.optimization_barrier((value, *others))


def reduce_and_gather(tiles, place):
    a, b, c = tiles

    def step(part, which, number):
        name = REDUCE[which][number]
        return halve(part, 2 if name == "zl" and number == 0 else 1, name, place)

    a, b = step(a, 0, 0), step(b, 1, 0)
    c, a = after(c, a)
    a, b, c = step(a, 0, 1), step(b, 1, 1), step(c, 2, 0)
    a = (a.astype(F32) + swap(a, "zh").astype(F32)).astype(BF16)
    c = step(c, 2, 1)
    b = (b.astype(F32) + swap(b, "zh").astype(F32)).astype(BF16)
    c = (c.astype(F32) + swap(c, "zh").astype(F32)).astype(BF16)
    parts = []
    for mine, order in zip((a, b, c), GATHER):
        mine = jnp.stack([mine, swap(mine, order[0])])
        held = [mine]
        for name in order[1:]:
            held = held + [swap(value, name) for value in held]
        parts += held + [swap(jnp.stack(held), "k")]
    return parts


def entry_kernel(acts_ref, momentum_ref, *refs):
    grads_refs, (new_ref, turned_ref) = refs[:BLOCKS], refs[-2:]
    grads = jnp.concatenate([ref[...] for ref in grads_refs])
    gradient = jnp.dot(acts_ref[...], grads, preferred_element_type=F32)
    momentum_new = 0.95 * momentum_ref[...] + gradient
    new_ref[...] = momentum_new
    turned_ref[...] = (gradient + 0.95 * momentum_new).T.astype(BF16)


def entry(acts_t, momentum, grads, first, held):
    rows, cols = momentum.shape
    tokens = acts_t.shape[1]
    width = cols // 9
    count = grads[0].shape[1] // width
    across = pl.BlockSpec((rows, width), lambda i: (0, first + i))
    return pl.pallas_call(
        entry_kernel,
        out_shape=(jax.ShapeDtypeStruct((rows, cols), F32), jax.ShapeDtypeStruct((count * width, rows), BF16)),
        grid=(count,),
        in_specs=[pl.BlockSpec((rows, tokens), lambda i: (0, 0)), across]
        + [pl.BlockSpec((value.shape[0], width), lambda i: (0, i)) for value in grads]
        + [pl.BlockSpec(memory_space=pl.ANY)] * len(held),
        out_specs=(across, pl.BlockSpec((width, rows), lambda i: (i, 0))),
        input_output_aliases={2 + len(grads): 0} if held else {},
        compiler_params=pltpu.CompilerParams(vmem_limit_bytes=40 * 2**20),
        cost_estimate=pl.CostEstimate(
            flops=2 * rows * count * width * tokens,
            bytes_accessed=rows * count * width * 10 + tokens * count * width * 2,
            transcendentals=0,
        ),
    )(acts_t, momentum, *grads, *held)


def finish_kernel(home_ref, weight_ref, update_ref, new_ref):
    update = home_ref[...].astype(F32).T
    update_ref[...] = update.astype(BF16)
    new_ref[...] = 0.998 * weight_ref[...] - 0.02 * update


def finish(home, weight):
    rows, cols = weight.shape
    width = cols // 9
    across = pl.BlockSpec((rows, width), lambda i: (0, i))
    return pl.pallas_call(
        finish_kernel,
        out_shape=(jax.ShapeDtypeStruct((rows, cols), BF16), jax.ShapeDtypeStruct((rows, cols), F32)),
        grid=(9,),
        in_specs=[pl.BlockSpec((width, rows), lambda i: (i, 0)), across],
        out_specs=(across, across),
        compiler_params=pltpu.CompilerParams(vmem_limit_bytes=40 * 2**20),
        cost_estimate=pl.CostEstimate(flops=4 * rows * cols, bytes_accessed=rows * cols * 12, transcendentals=0),
    )(home, weight)


def apply_near(source, tiles, total, blocks, first, last):
    rows = total.shape[2]
    depth = (last - first) * rows

    def near(b, _):
        start = pl.multiple_of((b + first) * rows, 128)
        own = pl.multiple_of(b * rows, 128)
        total[b] += jnp.dot(
            source[:, pl.ds(start, depth)],
            tiles[b, first:last].reshape(depth, rows),
            preferred_element_type=F32,
        )
        for d in range(max(first, 1), last):
            total[lax.rem(b + d, BLOCKS)] += lax.dot_general(
                source[:, pl.ds(own, rows)],
                tiles[b, d].reshape(rows, rows),
                (((1,), (1,)), ((), ())),
                preferred_element_type=F32,
            )
        return 0

    lax.fori_loop(*blocks, near, 0)


def apply_far(source, fours, total):
    rows = total.shape[2]

    def far(b, _):
        start = pl.multiple_of(b * rows, 128)
        other = pl.multiple_of((b + 4) * rows, 128)
        tile = fours[b].reshape(rows, rows)
        total[b] += jnp.dot(source[:, pl.ds(other, rows)], tile, preferred_element_type=F32)
        total[b + 4] += lax.dot_general(
            source[:, pl.ds(start, rows)], tile, (((1,), (1,)), ((), ())), preferred_element_type=F32
        )
        return 0

    lax.fori_loop(0, BLOCKS // 2, far, 0)


def load_tiles(place, part, pieces, tiles, fours, sem):
    for index in range(8):
        for inner in range(2):
            flips = (inner, index & 1, (index >> 1) & 1, index >> 2)
            there = {
                name: 1 - place[name] if flip else place[name] for name, flip in zip(GATHER[part] + ("k",), flips)
            }
            b = 2 * there["x"] + there["k"]
            e = 2 * there["y"] + there["zl"]
            piece = pieces[index].at[inner] if index < 4 else pieces[4].at[index - 4, inner]
            if part < 2:
                pltpu.make_async_copy(piece, tiles.at[b + 4 * part, pl.ds(0, 3), e], sem.at[part]).start()
            else:
                pltpu.make_async_copy(piece.at[0], tiles.at[b, 3, e], sem.at[2]).start()
                pltpu.make_async_copy(piece.at[1], tiles.at[b + 4, 3, e], sem.at[2]).start()
                pltpu.make_async_copy(piece.at[2], fours.at[b, e], sem.at[3]).start()
    if part < 2:
        block = tiles.at[pl.ds(4 * part, 4), pl.ds(0, 3)]
        return [pltpu.make_async_copy(block, block, sem.at[part])]
    block = tiles.at[:, 3]
    return [pltpu.make_async_copy(block, block, sem.at[2]), pltpu.make_async_copy(fours, fours, sem.at[3])]


def load_columns(place, panel_ref, source, sem):
    width = source.shape[0]
    rows = panel_ref.shape[2]
    group = 2 * place["x"]
    copies = []
    for b in range(BLOCKS + 3):
        j = lax.rem(b - group + 2 * BLOCKS, BLOCKS)
        for which, (first, last) in enumerate(STRIPS):
            ninth = width // 9
            start = pl.multiple_of((2 * first + place["x"] * (last - first)) * ninth, 16)
            block = panel_ref.at[j, pl.ds(start, (last - first) * ninth)]
            there = source.at[pl.ds(first * ninth, (last - first) * ninth), pl.ds(b * rows, rows)]
            copies.append(pltpu.make_async_copy(block, there, sem.at[len(STRIPS) * b + which]))
            copies[-1].start()
    return copies


def places_of(place_ref):
    return {name: place_ref[i] for i, name in enumerate(("x", "k", "y", "zh", "zl"))}


def product_kernel(place_ref, panel_ref, *refs):
    parts, (y_ref, z_ref, dot_ref), scratch = refs[: 3 * PIECES], refs[3 * PIECES : 3 * PIECES + 3], refs[3 * PIECES + 3 :]
    source, tiles, fours, total, tile_sem, x_sem, out_sem = scratch
    rows = total.shape[2]
    place = places_of(place_ref)
    columns = load_columns(place, panel_ref, source, x_sem)
    arrivals = [
        load_tiles(place, part, parts[PIECES * part : PIECES * part + PIECES], tiles, fours, tile_sem)
        for part in range(3)
    ]
    total[...] = jnp.zeros_like(total)
    for wait in columns + arrivals[0]:
        wait.wait()
    apply_near(source, tiles, total, (0, 4), 0, 3)
    for wait in arrivals[1]:
        wait.wait()
    apply_near(source, tiles, total, (4, 8), 0, 3)
    for wait in arrivals[2]:
        wait.wait()
    apply_near(source, tiles, total, (0, BLOCKS), 3, 4)
    apply_far(source, fours, total)
    out = pltpu.make_async_copy(total, y_ref, out_sem)
    out.start()
    for b in range(BLOCKS + 3):
        source[:, b * rows : (b + 1) * rows] = total[b % BLOCKS].astype(BF16)
    out.wait()
    total[...] = jnp.zeros_like(total)
    apply_near(source, tiles, total, (0, BLOCKS), 0, 4)
    apply_far(source, fours, total)
    out = pltpu.make_async_copy(total, z_ref, out_sem)
    out.start()
    lanes = jnp.zeros((1, rows), F32)
    for b in range(BLOCKS):
        lanes += jnp.sum(source[:, b * rows : (b + 1) * rows].astype(F32) * total[b], axis=0, keepdims=True)
    dot_ref[...] = jnp.broadcast_to(lanes, dot_ref.shape)
    out.wait()


def products(place, panel, parts):
    blocks, quarter, rows = panel.shape
    width = quarter // 2
    e = rows // 4
    anywhere = pl.BlockSpec(memory_space=pl.ANY)
    whole = jax.ShapeDtypeStruct((blocks, width, rows), F32)
    return pl.pallas_call(
        product_kernel,
        out_shape=(whole, whole, jax.ShapeDtypeStruct((8, rows), F32)),
        in_specs=[pl.BlockSpec(memory_space=pltpu.SMEM)] + [anywhere] * (1 + len(parts)),
        out_specs=(anywhere, anywhere, pl.BlockSpec(memory_space=pltpu.VMEM)),
        scratch_shapes=[
            pltpu.VMEM((width, (blocks + 3) * rows), BF16),
            pltpu.VMEM((blocks, 4, 4, e, rows), BF16),
            pltpu.VMEM((blocks // 2, 4, e, rows), BF16),
            pltpu.VMEM((blocks, width, rows), F32),
            pltpu.SemaphoreType.DMA((4,)),
            pltpu.SemaphoreType.DMA((len(STRIPS) * (blocks + 3),)),
            pltpu.SemaphoreType.DMA,
        ],
        compiler_params=pltpu.CompilerParams(vmem_limit_bytes=60 * 2**20),
        cost_estimate=pl.CostEstimate(
            flops=2 * 2 * 64 * width * rows * rows, bytes_accessed=2 * 36 * rows * rows, transcendentals=0
        ),
    )(place, panel, *parts)


def fast_body(acts, out_grads, momentum, weight):
    row, col = lax.axis_index("row"), lax.axis_index("col")
    z, x, y, core = row // 2, row % 2, col // 2, col % 2
    place = {"x": x, "k": core, "y": y, "zh": z // 2, "zl": z % 2}
    rows, cols = momentum.shape
    quarter = cols // 4
    half = quarter // 2
    e = rows // 4
    group = 2 * x

    token_acts = jnp.zeros((4, *acts.shape), BF16)
    for bit in range(4):
        value = lax.ppermute(acts, "col", [(i, i ^ bit) for i in range(4)]) if bit else acts
        token_acts = lax.dynamic_update_slice(token_acts, value[None], (col ^ bit, 0, 0))
    token_acts = token_acts.reshape(BLOCKS, -1, rows)
    acts_t = jnp.concatenate([take(token_acts, 0, row ^ bits) for bits in (0, 2, 4, 6, 1, 3, 5, 7)]).T

    panel = jnp.zeros((BLOCKS, quarter, rows), BF16)
    ninth = cols // 9
    held = ()
    for first, last in STRIPS:
        along = {0: out_grads[:, first * ninth : last * ninth]}
        along |= {2: swap(along[0], "zl"), 4: swap(along[0], "zh")}
        along[6] = swap(along[4], "zl")
        along |= {bits + 1: swap(value, "x") for bits, value in along.items()}
        momentum_new, turned = entry(acts_t, momentum, list(along.values()), first, held)
        held = (momentum_new,)
        share = (last - first) * ninth // 4
        start = first * ninth // 4
        pieces = turned.reshape(4, share, rows)
        for step in range(4):
            piece = take(pieces, 0, (z + step) % 4)
            if step:
                piece = row_shift(piece, 2 * step)
            source = 2 * ((z - step + 4) % 4)
            beside = swap(piece, "x")
            for block, value in ((source + x, piece), (source + 1 - x, beside)):
                j = (block - group + 8) % 8
                panel = lax.dynamic_update_slice(panel, value[None], (j, start, 0))
    deep = panel

    def tile(deep, i, j):
        return lax.dot_general(deep[i], deep[j], (((0,), (0,)), ((), ())), preferred_element_type=F32).astype(BF16)

    wanted = (((0, 0), (1, 0), (2, 0)), ((4, 4), (5, 4), (6, 4)), ((3, 0), (7, 4), (4, 0)))
    parts = []
    for which in range(3):
        if which == 2:
            deep, parts[0] = after(deep, parts[0])
        tiles = [tile(deep, (i + k) % BLOCKS, j + k) for k in range(2) for i, j in wanted[which]]
        tiles = jnp.stack(tiles).reshape(2, 3, 2, 2, e, rows)
        deep, tiles = after(deep, tiles)
        parts.append(halve(tiles, 0, "k", place))
    parts = reduce_and_gather(parts, place)

    places = jnp.stack([place[name] for name in ("x", "k", "y", "zh", "zl")]).astype(jnp.int32)
    one, two, lanes = products(places, panel, parts)
    total_sum = jnp.broadcast_to(jnp.sum(lanes[0]), (8, 128))
    total_sum = total_sum + sum(row_shift(total_sum, step) for step in range(1, 8))
    total_sum = total_sum + sum(
        lax.ppermute(total_sum, "col", [(i, i ^ bit) for i in range(4)]) for bit in range(1, 4)
    )
    schatten = jnp.sqrt(total_sum[0, 0] + 1e-06)
    square_root = jnp.sqrt(schatten)
    scale = math.sqrt(rows * BLOCKS) / jnp.sqrt(square_root)

    home = jnp.zeros((cols, rows), BF16)
    own = []
    for first, last in STRIPS:
        share = (last - first) * ninth // 8
        start = 2 * (first * ninth // 8) + x * share
        own.append(lax.dynamic_slice(panel, (0, start, 0), (BLOCKS, share, rows)))
    own = jnp.concatenate(own, axis=1)
    for step in range(BLOCKS):
        there = (row + step) % 8
        value = (
            3.4445 * take(own, 0, (there - group + 8) % 8).astype(F32)
            - (4.775 / square_root) * take(one, 0, there)
            + (2.0315 / schatten) * take(two, 0, there)
        )
        value = (scale * value).astype(BF16)
        if step:
            value = row_shift(value, step)
        for first, last in STRIPS:
            share = (last - first) * ninth // 8
            low = first * ninth // 8
            there = first * ninth + (row - step + 8) % 8 * share
            home = lax.dynamic_update_slice(home, value[low : low + share], (there, 0))
    update, weight_new = finish(home, weight)
    return (momentum_new, update, weight_new)


def solution(mesh):
    spec = P("row", "col")
    in_specs = (P("col", "row"), spec, spec, spec)
    fast = mesh.shape["row"] == 8 and mesh.shape["col"] == 4
    body = fast_body if fast else general_body
    return jax.shard_map(body, mesh=mesh, in_specs=in_specs, out_specs=(spec, spec, spec), check_vma=False)
```

```python
import functools
import math

import jax
import jax.numpy as jnp
from jax import lax
from jax.experimental import pallas as pl
from jax.experimental.pallas import tpu as pltpu
from jax.sharding import PartitionSpec as P

F32 = jnp.float32
BF16 = jnp.bfloat16


def general_body(acts, out_grads, momentum, weight):
    token_acts = lax.all_gather(acts, "col", axis=0, tiled=True)
    token_grads = lax.all_gather(out_grads, "row", axis=0, tiled=True)
    gradient = lax.dot_general(token_acts, token_grads, (((0,), (0,)), ((), ())), preferred_element_type=F32)
    momentum_new = 0.95 * momentum + gradient
    blended = gradient + 0.95 * momentum_new
    rounded = blended.astype(BF16)
    col_panel = lax.all_gather(rounded, "row", axis=0, tiled=True)
    gram_tile = lax.psum_scatter(
        lax.dot_general(col_panel, rounded, (((1,), (1,)), ((), ())), preferred_element_type=F32).astype(BF16),
        "col",
        scatter_dimension=0,
        tiled=True,
    )
    gram_cols = lax.all_gather(gram_tile, "col", axis=0, tiled=True)
    gram_rows = lax.all_gather(gram_tile, "row", axis=1, tiled=True)
    gram_square = jnp.dot(gram_rows, gram_cols, preferred_element_type=F32)
    total_sum = lax.psum(jnp.sum(gram_square * gram_square), ("row", "col"))
    schatten = jnp.sqrt(total_sum + 1e-06)
    square_root = jnp.sqrt(schatten)
    fourth_root = jnp.sqrt(square_root)
    poly_tile = (-4.775 * gram_tile.astype(F32) / square_root + 2.0315 * gram_square / schatten).astype(BF16)
    poly_cols = lax.all_gather(poly_tile, "col", axis=0, tiled=True)
    product = lax.dot_general(poly_cols, col_panel, (((0,), (0,)), ((), ())), preferred_element_type=F32)
    orthogonal = (3.4445 * rounded.astype(F32) + product) / fourth_root
    factor = math.sqrt(col_panel.shape[0])
    update = (factor * orthogonal).astype(BF16)
    weight_new = 0.998 * weight - 0.02 * factor * orthogonal
    return (momentum_new, update, weight_new)


BLOCKS = 8
STRIPS = ((0, 4), (4, 9))
PIECES = 5
MOVES = {"x": ("row", 1), "zl": ("row", 2), "zh": ("row", 4), "y": ("col", 2), "k": ("col", 1)}
REDUCE = (("y", "zl"), ("zl", "y"), ("zl", "y"))
GATHER = (("x", "y", "zl"), ("zl", "y", "x"), ("zl", "x", "y"))


def row_shift(value, step):
    return lax.ppermute(value, "row", [(i, (i + step) % BLOCKS) for i in range(BLOCKS)])


def swap(value, name):
    axis, bit = MOVES[name]
    size = 8 if axis == "row" else 4
    return lax.ppermute(value, axis, [(i, i ^ bit) for i in range(size)])


def take(value, dim, index):
    return lax.dynamic_index_in_dim(value, index, dim, keepdims=False)


def halve(tiles, dim, name, place):
    received = swap(take(tiles, dim, 1 - place[name]), name)
    return (take(tiles, dim, place[name]).astype(F32) + received.astype(F32)).astype(BF16)


def after(value, *others):
    return lax.optimization_barrier((value, *others))


def reduce_and_gather(tiles, place):
    a, b, c = tiles

    def step(part, which, number):
        name = REDUCE[which][number]
        return halve(part, 2 if name == "zl" and number == 0 else 1, name, place)

    a, b = step(a, 0, 0), step(b, 1, 0)
    c, a = after(c, a)
    a, b, c = step(a, 0, 1), step(b, 1, 1), step(c, 2, 0)
    a = (a.astype(F32) + swap(a, "zh").astype(F32)).astype(BF16)
    c = step(c, 2, 1)
    b = (b.astype(F32) + swap(b, "zh").astype(F32)).astype(BF16)
    c = (c.astype(F32) + swap(c, "zh").astype(F32)).astype(BF16)
    parts = []
    for mine, order in zip((a, b, c), GATHER):
        mine = jnp.stack([mine, swap(mine, order[0])])
        held = [mine]
        for name in order[1:]:
            held = held + [swap(value, name) for value in held]
        parts += held + [swap(jnp.stack(held), "k")]
    return parts


def entry_kernel(acts_ref, momentum_ref, *refs):
    grads_refs, (new_ref, turned_ref) = refs[:BLOCKS], refs[-2:]
    grads = jnp.concatenate([ref[...] for ref in grads_refs])
    gradient = jnp.dot(acts_ref[...], grads, preferred_element_type=F32)
    momentum_new = 0.95 * momentum_ref[...] + gradient
    new_ref[...] = momentum_new
    turned_ref[...] = (gradient + 0.95 * momentum_new).T.astype(BF16)


def entry(acts_t, momentum, grads, first, held):
    rows, cols = momentum.shape
    tokens = acts_t.shape[1]
    width = cols // 9
    count = grads[0].shape[1] // width
    across = pl.BlockSpec((rows, width), lambda i: (0, first + i))
    return pl.pallas_call(
        entry_kernel,
        out_shape=(jax.ShapeDtypeStruct((rows, cols), F32), jax.ShapeDtypeStruct((count * width, rows), BF16)),
        grid=(count,),
        in_specs=[pl.BlockSpec((rows, tokens), lambda i: (0, 0)), across]
        + [pl.BlockSpec((value.shape[0], width), lambda i: (0, i)) for value in grads]
        + [pl.BlockSpec(memory_space=pl.ANY)] * len(held),
        out_specs=(across, pl.BlockSpec((width, rows), lambda i: (i, 0))),
        input_output_aliases={2 + len(grads): 0} if held else {},
        compiler_params=pltpu.CompilerParams(vmem_limit_bytes=40 * 2**20),
        cost_estimate=pl.CostEstimate(
            flops=2 * rows * count * width * tokens,
            bytes_accessed=rows * count * width * 10 + tokens * count * width * 2,
            transcendentals=0,
        ),
    )(acts_t, momentum, *grads, *held)


def finish_kernel(home_ref, weight_ref, update_ref, new_ref):
    update = home_ref[...].astype(F32).T
    update_ref[...] = update.astype(BF16)
    new_ref[...] = 0.998 * weight_ref[...] - 0.02 * update


def finish(home, weight):
    rows, cols = weight.shape
    width = cols // 9
    across = pl.BlockSpec((rows, width), lambda i: (0, i))
    return pl.pallas_call(
        finish_kernel,
        out_shape=(jax.ShapeDtypeStruct((rows, cols), BF16), jax.ShapeDtypeStruct((rows, cols), F32)),
        grid=(9,),
        in_specs=[pl.BlockSpec((width, rows), lambda i: (i, 0)), across],
        out_specs=(across, across),
        compiler_params=pltpu.CompilerParams(vmem_limit_bytes=40 * 2**20),
        cost_estimate=pl.CostEstimate(flops=4 * rows * cols, bytes_accessed=rows * cols * 12, transcendentals=0),
    )(home, weight)


def apply_near(source, tiles, total, blocks, first, last):
    rows = total.shape[2]
    depth = (last - first) * rows

    def near(b, _):
        start = pl.multiple_of((b + first) * rows, 128)
        own = pl.multiple_of(b * rows, 128)
        total[b] += jnp.dot(
            source[:, pl.ds(start, depth)],
            tiles[b, first:last].reshape(depth, rows),
            preferred_element_type=F32,
        )
        for d in range(max(first, 1), last):
            total[lax.rem(b + d, BLOCKS)] += lax.dot_general(
                source[:, pl.ds(own, rows)],
                tiles[b, d].reshape(rows, rows),
                (((1,), (1,)), ((), ())),
                preferred_element_type=F32,
            )
        return 0

    lax.fori_loop(*blocks, near, 0)


def apply_all(source, tiles, total):
    rows = total.shape[2]

    def straight(b, _):
        start = pl.multiple_of(b * rows, 128)
        total[b] = jnp.dot(
            source[:, pl.ds(start, 4 * rows)], tiles[b].reshape(4 * rows, rows), preferred_element_type=F32
        )
        return 0

    def turned(b, _):
        start = pl.multiple_of(b * rows, 128)
        for d in range(1, 4):
            total[lax.rem(b + d, BLOCKS)] += lax.dot_general(
                source[:, pl.ds(start, rows)],
                tiles[b, d].reshape(rows, rows),
                (((1,), (1,)), ((), ())),
                preferred_element_type=F32,
            )
        return 0

    lax.fori_loop(0, BLOCKS, straight, 0)
    lax.fori_loop(0, BLOCKS, turned, 0)


def apply_far(source, fours, total):
    rows = total.shape[2]

    def far(b, _):
        start = pl.multiple_of(b * rows, 128)
        other = pl.multiple_of((b + 4) * rows, 128)
        tile = fours[b].reshape(rows, rows)
        total[b] += jnp.dot(source[:, pl.ds(other, rows)], tile, preferred_element_type=F32)
        total[b + 4] += lax.dot_general(
            source[:, pl.ds(start, rows)], tile, (((1,), (1,)), ((), ())), preferred_element_type=F32
        )
        return 0

    lax.fori_loop(0, BLOCKS // 2, far, 0)


def load_tiles(place, part, pieces, tiles, fours, sem):
    for index in range(8):
        for inner in range(2):
            flips = (inner, index & 1, (index >> 1) & 1, index >> 2)
            there = {
                name: 1 - place[name] if flip else place[name] for name, flip in zip(GATHER[part] + ("k",), flips)
            }
            b = 2 * there["x"] + there["k"]
            e = 2 * there["y"] + there["zl"]
            piece = pieces[index].at[inner] if index < 4 else pieces[4].at[index - 4, inner]
            if part < 2:
                pltpu.make_async_copy(piece, tiles.at[b + 4 * part, pl.ds(0, 3), e], sem.at[part]).start()
            else:
                pltpu.make_async_copy(piece.at[0], tiles.at[b, 3, e], sem.at[2]).start()
                pltpu.make_async_copy(piece.at[1], tiles.at[b + 4, 3, e], sem.at[2]).start()
                pltpu.make_async_copy(piece.at[2], fours.at[b, e], sem.at[3]).start()
    if part < 2:
        block = tiles.at[pl.ds(4 * part, 4), pl.ds(0, 3)]
        return [pltpu.make_async_copy(block, block, sem.at[part])]
    block = tiles.at[:, 3]
    return [pltpu.make_async_copy(block, block, sem.at[2]), pltpu.make_async_copy(fours, fours, sem.at[3])]


def load_columns(place, panel_ref, source, sem):
    width = source.shape[0]
    rows = panel_ref.shape[2]
    group = 2 * place["x"]
    copies = []
    for b in range(BLOCKS + 3):
        j = lax.rem(b - group + 2 * BLOCKS, BLOCKS)
        for which, (first, last) in enumerate(STRIPS):
            ninth = width // 9
            start = pl.multiple_of((2 * first + place["x"] * (last - first)) * ninth, 16)
            block = panel_ref.at[j, pl.ds(start, (last - first) * ninth)]
            there = source.at[pl.ds(first * ninth, (last - first) * ninth), pl.ds(b * rows, rows)]
            copies.append(pltpu.make_async_copy(block, there, sem.at[len(STRIPS) * b + which]))
            copies[-1].start()
    return copies


def places_of(place_ref):
    return {name: place_ref[i] for i, name in enumerate(("x", "k", "y", "zh", "zl"))}


def product_kernel(place_ref, panel_ref, *refs):
    parts, (y_ref, z_ref, dot_ref), scratch = refs[: 3 * PIECES], refs[3 * PIECES : 3 * PIECES + 3], refs[3 * PIECES + 3 :]
    source, tiles, fours, total, tile_sem, x_sem, out_sem = scratch
    rows = total.shape[2]
    place = places_of(place_ref)
    columns = load_columns(place, panel_ref, source, x_sem)
    arrivals = [
        load_tiles(place, part, parts[PIECES * part : PIECES * part + PIECES], tiles, fours, tile_sem)
        for part in range(3)
    ]
    total[...] = jnp.zeros_like(total)
    for wait in columns + arrivals[0]:
        wait.wait()
    apply_near(source, tiles, total, (0, 4), 0, 3)
    for wait in arrivals[1]:
        wait.wait()
    apply_near(source, tiles, total, (4, 8), 0, 3)
    for wait in arrivals[2]:
        wait.wait()
    apply_near(source, tiles, total, (0, BLOCKS), 3, 4)
    apply_far(source, fours, total)
    out = pltpu.make_async_copy(total, y_ref, out_sem)
    out.start()
    for b in range(BLOCKS + 3):
        source[:, b * rows : (b + 1) * rows] = total[b % BLOCKS].astype(BF16)
    out.wait()
    apply_all(source, tiles, total)
    apply_far(source, fours, total)
    out = pltpu.make_async_copy(total, z_ref, out_sem)
    out.start()
    lanes = jnp.zeros((1, rows), F32)
    for b in range(BLOCKS):
        lanes += jnp.sum(source[:, b * rows : (b + 1) * rows].astype(F32) * total[b], axis=0, keepdims=True)
    dot_ref[...] = jnp.broadcast_to(lanes, dot_ref.shape)
    out.wait()


def products(place, panel, parts):
    blocks, quarter, rows = panel.shape
    width = quarter // 2
    e = rows // 4
    anywhere = pl.BlockSpec(memory_space=pl.ANY)
    whole = jax.ShapeDtypeStruct((blocks, width, rows), F32)
    return pl.pallas_call(
        product_kernel,
        out_shape=(whole, whole, jax.ShapeDtypeStruct((8, rows), F32)),
        in_specs=[pl.BlockSpec(memory_space=pltpu.SMEM)] + [anywhere] * (1 + len(parts)),
        out_specs=(anywhere, anywhere, pl.BlockSpec(memory_space=pltpu.VMEM)),
        scratch_shapes=[
            pltpu.VMEM((width, (blocks + 3) * rows), BF16),
            pltpu.VMEM((blocks, 4, 4, e, rows), BF16),
            pltpu.VMEM((blocks // 2, 4, e, rows), BF16),
            pltpu.VMEM((blocks, width, rows), F32),
            pltpu.SemaphoreType.DMA((4,)),
            pltpu.SemaphoreType.DMA((len(STRIPS) * (blocks + 3),)),
            pltpu.SemaphoreType.DMA,
        ],
        compiler_params=pltpu.CompilerParams(vmem_limit_bytes=60 * 2**20),
        cost_estimate=pl.CostEstimate(
            flops=2 * 2 * 64 * width * rows * rows, bytes_accessed=2 * 36 * rows * rows, transcendentals=0
        ),
    )(place, panel, *parts)


def fast_body(acts, out_grads, momentum, weight):
    row, col = lax.axis_index("row"), lax.axis_index("col")
    z, x, y, core = row // 2, row % 2, col // 2, col % 2
    place = {"x": x, "k": core, "y": y, "zh": z // 2, "zl": z % 2}
    rows, cols = momentum.shape
    quarter = cols // 4
    half = quarter // 2
    e = rows // 4
    group = 2 * x

    token_acts = jnp.zeros((4, *acts.shape), BF16)
    for bit in range(4):
        value = lax.ppermute(acts, "col", [(i, i ^ bit) for i in range(4)]) if bit else acts
        token_acts = lax.dynamic_update_slice(token_acts, value[None], (col ^ bit, 0, 0))
    token_acts = token_acts.reshape(BLOCKS, -1, rows)
    acts_t = jnp.concatenate([take(token_acts, 0, row ^ bits) for bits in (0, 2, 4, 6, 1, 3, 5, 7)]).T

    panel = jnp.zeros((BLOCKS, quarter, rows), BF16)
    ninth = cols // 9
    held = ()
    for first, last in STRIPS:
        along = {0: out_grads[:, first * ninth : last * ninth]}
        along |= {2: swap(along[0], "zl"), 4: swap(along[0], "zh")}
        along[6] = swap(along[4], "zl")
        along |= {bits + 1: swap(value, "x") for bits, value in along.items()}
        momentum_new, turned = entry(acts_t, momentum, list(along.values()), first, held)
        held = (momentum_new,)
        share = (last - first) * ninth // 4
        start = first * ninth // 4
        pieces = turned.reshape(4, share, rows)
        for step in range(4):
            piece = take(pieces, 0, (z + step) % 4)
            if step:
                piece = row_shift(piece, 2 * step)
            source = 2 * ((z - step + 4) % 4)
            beside = swap(piece, "x")
            for block, value in ((source + x, piece), (source + 1 - x, beside)):
                j = (block - group + 8) % 8
                panel = lax.dynamic_update_slice(panel, value[None], (j, start, 0))
    deep = panel

    def tile(deep, i, j):
        return lax.dot_general(deep[i], deep[j], (((0,), (0,)), ((), ())), preferred_element_type=F32).astype(BF16)

    wanted = (((0, 0), (1, 0), (2, 0)), ((4, 4), (5, 4), (6, 4)), ((3, 0), (7, 4), (4, 0)))
    parts = []
    for which in range(3):
        if which == 2:
            deep, parts[0] = after(deep, parts[0])
        tiles = [tile(deep, (i + k) % BLOCKS, j + k) for k in range(2) for i, j in wanted[which]]
        tiles = jnp.stack(tiles).reshape(2, 3, 2, 2, e, rows)
        deep, tiles = after(deep, tiles)
        parts.append(halve(tiles, 0, "k", place))
    parts = reduce_and_gather(parts, place)

    places = jnp.stack([place[name] for name in ("x", "k", "y", "zh", "zl")]).astype(jnp.int32)
    one, two, lanes = products(places, panel, parts)
    total_sum = jnp.broadcast_to(jnp.sum(lanes[0]), (8, 128))
    total_sum = total_sum + sum(row_shift(total_sum, step) for step in range(1, 8))
    total_sum = total_sum + sum(
        lax.ppermute(total_sum, "col", [(i, i ^ bit) for i in range(4)]) for bit in range(1, 4)
    )
    schatten = jnp.sqrt(total_sum[0, 0] + 1e-06)
    square_root = jnp.sqrt(schatten)
    scale = math.sqrt(rows * BLOCKS) / jnp.sqrt(square_root)

    home = jnp.zeros((cols, rows), BF16)
    own = []
    for first, last in STRIPS:
        share = (last - first) * ninth // 8
        start = 2 * (first * ninth // 8) + x * share
        own.append(lax.dynamic_slice(panel, (0, start, 0), (BLOCKS, share, rows)))
    own = jnp.concatenate(own, axis=1)
    for step in range(BLOCKS):
        there = (row + step) % 8
        value = (
            3.4445 * take(own, 0, (there - group + 8) % 8).astype(F32)
            - (4.775 / square_root) * take(one, 0, there)
            + (2.0315 / schatten) * take(two, 0, there)
        )
        value = (scale * value).astype(BF16)
        if step:
            value = row_shift(value, step)
        for first, last in STRIPS:
            share = (last - first) * ninth // 8
            low = first * ninth // 8
            there = first * ninth + (row - step + 8) % 8 * share
            home = lax.dynamic_update_slice(home, value[low : low + share], (there, 0))
    update, weight_new = finish(home, weight)
    return (momentum_new, update, weight_new)


def solution(mesh):
    spec = P("row", "col")
    in_specs = (P("col", "row"), spec, spec, spec)
    fast = mesh.shape["row"] == 8 and mesh.shape["col"] == 4
    body = fast_body if fast else general_body
    return jax.shard_map(body, mesh=mesh, in_specs=in_specs, out_specs=(spec, spec, spec), check_vma=False)
```
